32 devices in a mesh: docs: 16 (over z, x, core), dims: 2 (over y).
Axes of the slice: x: 2, y: 2, z: 4, core: 2. Of those that a mesh axis runs over, the one named last changes fastest.
Arguments:
- queries: bfloat16 [8192, 3072], P('docs', 'dims'), may hold values from -6 to 6
- doc_vectors: bfloat16 [32768, 3072], P('docs', 'dims'), may hold values from -6 to 6
- surv_pairs: int32 [16, 144], P('docs'), may hold values from 0 to 1023
- surv_count: int32 [16], P('docs'), may hold values from 36 to 144, as said below
- short_pairs: int32 [16, 96], P('docs'), may hold values from 0 to 1023
- short_count: int32 [16], P('docs'), may hold values from 24 to 96, as said below
Outputs:
- prefix_scores: float32 [16, 144, 128, 128], P('docs', None, 'dims')
- full_scores: float32 [16, 96, 128, 128], P('docs', None, 'dims')
The draws below stay inside these ranges and needn't reach their ends.
Inputs may be any that keep to these rules, and one draw needn't show every extreme that they name: `surv_count`: each shard's live survivor slots; some shard has all 144 slots live. `short_count`: each shard's live shortlist slots; some shard has all 96 slots live.
All inputs are finite; a program needn't handle non-finite values.
Results may differ from the reference program's by a relative error of at most 0.0003.
Values may be sent and summed in bfloat16 or wider, within the bound.
A program may use at most 256 MiB of HBM per device.

```python
import jax
import jax.numpy as jnp
from jax import lax

D = 3072
PREFIX = 768
QB = 128
DB = 128
SCAP = 144
CAP = 96
SLICE = 1536
QUERIES = 8192
QBLK = 64
DOCS = 32768
DBLK_DEV = 16
N_DOCS = 16
N_DIMS = 2


def live_counts(key, capacity):
    counts = jax.random.randint(jax.random.fold_in(key, 1), (N_DOCS,), capacity // 4, capacity + 1)
    full_at = jax.random.randint(jax.random.fold_in(key, 2), (), 0, N_DOCS)
    return jnp.where(jnp.arange(N_DOCS) == full_at, capacity, counts).astype(jnp.int32)


def draw_surv_count(key, part):
    return live_counts(jax.random.fold_in(key, 11), SCAP)


def draw_short_count(key, part):
    return live_counts(jax.random.fold_in(key, 23), CAP)


def with_ends(entries, key, low, high):
    place = [jax.random.randint(jax.random.fold_in(key, axis), (), 0, length) for axis, length in enumerate(entries.shape)]
    widest = entries.shape.index(max(entries.shape))
    beside = place[:widest] + [(place[widest] + 1) % entries.shape[widest]] + place[widest + 1:]
    return entries.at[tuple(place)].set(low).at[tuple(beside)].set(high)


def steps_of(stream_key, shape, cuts, smallest, high):
    level = 1.0
    for dim, shards_of in cuts:
        draws = jax.random.uniform(jax.random.fold_in(jax.random.fold_in(stream_key, 6), dim), (shards_of,), jnp.float32, smallest / len(cuts), high / len(cuts))
        level = level * jnp.repeat(jnp.exp(draws), shape[dim] // shards_of).reshape((-1,) + (1,) * (len(shape) - 1 - dim))
    return level


def normal_values(rng, dims, scale, reach, cuts=(), kind=jnp.bfloat16):
    level = steps_of(rng, dims, cuts, -0.22, 0.18) if cuts else 1.0
    drawn = jax.random.normal(rng, dims, jnp.float32) * scale * level
    return jnp.minimum(jnp.maximum(drawn, -reach), reach).astype(kind)


def setup_inputs(seed: int = 0) -> dict:
    splits = jax.random.split(jax.random.key(seed), 7)
    queries = normal_values(splits[0], (QUERIES, D), 1.0, 6.0, ((0, 16), (1, 2)))
    doc_vectors = normal_values(splits[1], (DOCS, D), 1.0, 6.0, ((0, 16), (1, 2)))
    surv_pairs = with_ends(jax.random.randint(splits[2], (N_DOCS, SCAP), 0, QBLK * DBLK_DEV), jax.random.fold_in(splits[2], 1), 0, (QBLK * DBLK_DEV) - 1).astype(jnp.int32)
    surv_count = draw_surv_count(jax.random.fold_in(splits[6], 71), 0)
    short_pairs = with_ends(jax.random.randint(splits[4], (N_DOCS, CAP), 0, QBLK * DBLK_DEV), jax.random.fold_in(splits[4], 1), 0, (QBLK * DBLK_DEV) - 1).astype(jnp.int32)
    short_count = draw_short_count(jax.random.fold_in(splits[6], 71), 0)
    return dict(queries=queries, doc_vectors=doc_vectors, surv_pairs=surv_pairs, surv_count=surv_count, short_pairs=short_pairs, short_count=short_count)


def shard_scores(query_blocks, doc_blocks, pair_list, live_count, prefix_only):
    picked_queries = query_blocks[pair_list // DBLK_DEV]
    picked_docs = doc_blocks[pair_list % DBLK_DEV]
    totals = jnp.zeros((pair_list.shape[0], QB, DB), jnp.float32)
    for slice_index in range(N_DIMS):
        column_start = slice_index * SLICE
        query_part = picked_queries[:, :, column_start:column_start + SLICE].astype(jnp.float32)
        doc_part = picked_docs[:, :, column_start:column_start + SLICE].astype(jnp.float32)
        if prefix_only:
            columns = column_start + jnp.arange(SLICE)
            doc_part = jnp.where(columns[None, None, :] < PREFIX, doc_part, jnp.float32(0.0))
        partial_term = jnp.einsum("sqc,sdc->sqd", query_part, doc_part)
        totals = totals + partial_term
    factor = float(PREFIX) ** -0.5 if prefix_only else float(D) ** -0.5
    slots = jnp.arange(pair_list.shape[0])
    return jnp.where(slots[:, None, None] < live_count, totals * factor, jnp.float32(0.0))


def reference(queries, doc_vectors, surv_pairs, surv_count, short_pairs, short_count):
    query_blocks = queries.reshape(QBLK, QB, D)
    doc_shards = doc_vectors.reshape(N_DOCS, DBLK_DEV, DB, D)

    def prefix_shard(packed):
        return shard_scores(query_blocks, packed[0], packed[1], packed[2], True)

    def full_shard(packed):
        return shard_scores(query_blocks, packed[0], packed[1], packed[2], False)

    prefix_scores = lax.map(prefix_shard, (doc_shards, surv_pairs, surv_count))
    full_scores = lax.map(full_shard, (doc_shards, short_pairs, short_count))
    return (prefix_scores, full_scores)
```

```python
import functools

import jax
import jax.numpy as jnp
from jax import lax
from jax.experimental import pallas as pl
from jax.experimental.pallas import tpu as pltpu
from jax.sharding import PartitionSpec as P

D = 3072
PREFIX = 768
QB = 128
DB = 128
STEPS = 12


def scores(
    n_dims, local_blocks, surv_ref, surv_n_ref, short_ref, short_n_ref, *refs
):
    query_hbm, doc_hbm = refs[:n_dims], refs[n_dims : 2 * n_dims]
    prefix_ref, full_ref, query_vmem, doc_vmem, query_sem, doc_sem = refs[2 * n_dims :]
    width = doc_vmem.shape[-1]
    step = pl.program_id(0)
    me = lax.axis_index("dims")

    @pl.when(step == 0)
    def _():
        copies = []
        for shift in range(n_dims):
            place = lax.rem(me - shift + n_dims, n_dims)
            copies.append(
                pltpu.make_async_copy(doc_hbm[shift], doc_vmem.at[place], doc_sem.at[shift])
            )
            copies.append(
                pltpu.make_async_copy(query_hbm[shift], query_vmem.at[place], query_sem.at[shift])
            )
        for copy in copies:
            copy.start()
        for copy in copies:
            copy.wait()

    def slots(pair_ref, count_ref, out_ref, columns):
        per_step = out_ref.shape[0]
        for i in range(per_step):
            slot = step * per_step + i
            pair = pair_ref[slot]
            query_block = pair // local_blocks
            doc_block = pair % local_blocks
            total = None
            for j in range(n_dims):
                used = min(max(columns - j * width, 0), width)
                if used == 0:
                    continue
                term = lax.dot_general(
                    query_vmem[j, query_block, :, :used],
                    doc_vmem[j, doc_block, :, :used],
                    (((1,), (1,)), ((), ())),
                    preferred_element_type=jnp.float32,
                )
                total = term if total is None else total + term
            scaled = total * (float(columns) ** -0.5)
            out_ref[i] = jnp.where(slot < count_ref[0], scaled, jnp.float32(0.0))

    slots(short_ref, short_n_ref, full_ref, D)
    slots(surv_ref, surv_n_ref, prefix_ref, PREFIX)


def shards(
    n_dims, queries, doc_vectors, surv_pairs, surv_count, short_pairs, short_count
):
    width = queries.shape[1]
    rows = QB // n_dims
    local_blocks = doc_vectors.shape[0] // DB
    me = lax.axis_index("dims")
    by_rows = queries.reshape(-1, n_dims, rows, width)
    docs = doc_vectors.reshape(local_blocks, DB, width)
    query_parts, doc_parts = [], []
    for shift in range(n_dims):
        target = lax.rem(me + shift, n_dims)
        part = lax.dynamic_index_in_dim(by_rows, target, 1, keepdims=False)
        doc_part = docs
        if shift:
            pairs = [(i, (i + shift) % n_dims) for i in range(n_dims)]
            part = lax.ppermute(part, "dims", pairs)
            doc_part = lax.ppermute(docs, "dims", pairs)
        query_parts.append(lax.all_gather(part, "docs", axis=0, tiled=True))
        doc_parts.append(doc_part)
    blocks = query_parts[0].shape[0]
    survivors, shortlist = surv_pairs.shape[1], short_pairs.shape[1]
    outs = [
        jax.ShapeDtypeStruct((survivors, rows, DB), jnp.float32),
        jax.ShapeDtypeStruct((shortlist, rows, DB), jnp.float32),
    ]
    moved = 2 * (blocks * rows + local_blocks * DB) * D + 4 * (survivors + shortlist) * rows * DB
    prefix_out, full_out = pl.pallas_call(
        functools.partial(scores, n_dims, local_blocks),
        out_shape=outs,
        grid_spec=pltpu.PrefetchScalarGridSpec(
            num_scalar_prefetch=4,
            grid=(STEPS,),
            in_specs=[pl.BlockSpec(memory_space=pl.ANY)] * (2 * n_dims),
            out_specs=[
                pl.BlockSpec((survivors // STEPS, rows, DB), lambda g, *_: (g, 0, 0)),
                pl.BlockSpec((shortlist // STEPS, rows, DB), lambda g, *_: (g, 0, 0)),
            ],
            scratch_shapes=[
                pltpu.VMEM((n_dims, blocks, rows, width), jnp.bfloat16),
                pltpu.VMEM((n_dims, local_blocks, DB, width), jnp.bfloat16),
                pltpu.SemaphoreType.DMA((n_dims,)),
                pltpu.SemaphoreType.DMA((n_dims,)),
            ],
        ),
        compiler_params=pltpu.CompilerParams(vmem_limit_bytes=56 * 2**20),
        cost_estimate=pl.CostEstimate(
            flops=2 * rows * DB * (shortlist * D + survivors * PREFIX),
            bytes_accessed=moved,
            transcendentals=0,
        ),
    )(surv_pairs[0], surv_count, short_pairs[0], short_count, *query_parts, *doc_parts)
    return (prefix_out[None], full_out[None])


def solution(mesh):
    placed = (
        P("docs", "dims"),
        P("docs", "dims"),
        P("docs", None),
        P("docs"),
        P("docs", None),
        P("docs"),
    )
    return jax.shard_map(
        functools.partial(shards, mesh.shape["dims"]),
        mesh=mesh,
        in_specs=placed,
        out_specs=(P("docs", None, "dims", None), P("docs", None, "dims", None)),
        check_vma=False,
    )
```

```python
import functools

import jax
import jax.numpy as jnp
from jax import lax
from jax.experimental import pallas as pl
from jax.experimental.pallas import tpu as pltpu
from jax.sharding import PartitionSpec as P

D = 3072
PREFIX = 768
QB = 128
DB = 128
STEPS = 12


def scores(
    n_dims, local_blocks, surv_ref, surv_n_ref, short_ref, short_n_ref, *refs
):
    query_hbm, doc_hbm = refs[0], refs[1 : 1 + n_dims]
    prefix_ref, full_ref, query_vmem, doc_vmem, query_sem, doc_sem = refs[1 + n_dims :]
    width = doc_vmem.shape[-1]
    per_shard = query_vmem.shape[2]
    step = pl.program_id(0)
    me = lax.axis_index("dims")

    @pl.when(step == 0)
    def _():
        copies = []
        for shift in range(n_dims):
            place = lax.rem(me - shift + n_dims, n_dims)
            copies.append(
                pltpu.make_async_copy(doc_hbm[shift], doc_vmem.at[place], doc_sem.at[shift])
            )
            copies.append(
                pltpu.make_async_copy(
                    query_hbm.at[:, shift], query_vmem.at[place], query_sem.at[shift]
                )
            )
        for copy in copies:
            copy.start()
        for copy in copies:
            copy.wait()

    def slots(pair_ref, count_ref, out_ref, columns):
        per_step = out_ref.shape[0]
        for i in range(per_step):
            slot = step * per_step + i
            pair = pair_ref[slot]
            query_block = pair // local_blocks
            doc_block = pair % local_blocks
            total = None
            for j in range(n_dims):
                used = min(max(columns - j * width, 0), width)
                if used == 0:
                    continue
                term = lax.dot_general(
                    query_vmem[j, query_block // per_shard, query_block % per_shard, :, :used],
                    doc_vmem[j, doc_block, :, :used],
                    (((1,), (1,)), ((), ())),
                    preferred_element_type=jnp.float32,
                )
                total = term if total is None else total + term
            scaled = total * (float(columns) ** -0.5)
            out_ref[i] = jnp.where(slot < count_ref[0], scaled, jnp.float32(0.0))

    slots(short_ref, short_n_ref, full_ref, D)
    slots(surv_ref, surv_n_ref, prefix_ref, PREFIX)


def shards(
    n_dims, queries, doc_vectors, surv_pairs, surv_count, short_pairs, short_count
):
    width = queries.shape[1]
    rows = QB // n_dims
    local_blocks = doc_vectors.shape[0] // DB
    me = lax.axis_index("dims")
    by_rows = queries.reshape(-1, n_dims, rows, width)
    docs = doc_vectors.reshape(local_blocks, DB, width)
    query_parts, doc_parts = [], []
    for shift in range(n_dims):
        target = lax.rem(me + shift, n_dims)
        part = lax.dynamic_index_in_dim(by_rows, target, 1, keepdims=False)
        doc_part = docs
        if shift:
            pairs = [(i, (i + shift) % n_dims) for i in range(n_dims)]
            part = lax.ppermute(part, "dims", pairs)
            doc_part = lax.ppermute(docs, "dims", pairs)
        query_parts.append(part)
        doc_parts.append(doc_part)
    every_query = lax.all_gather(jnp.stack(query_parts), "docs", axis=0, tiled=False)
    n_docs, _, per_shard = every_query.shape[:3]
    blocks = n_docs * per_shard
    survivors, shortlist = surv_pairs.shape[1], short_pairs.shape[1]
    outs = [
        jax.ShapeDtypeStruct((survivors, rows, DB), jnp.float32),
        jax.ShapeDtypeStruct((shortlist, rows, DB), jnp.float32),
    ]
    moved = 2 * (blocks * rows + local_blocks * DB) * D + 4 * (survivors + shortlist) * rows * DB
    prefix_out, full_out = pl.pallas_call(
        functools.partial(scores, n_dims, local_blocks),
        out_shape=outs,
        grid_spec=pltpu.PrefetchScalarGridSpec(
            num_scalar_prefetch=4,
            grid=(STEPS,),
            in_specs=[pl.BlockSpec(memory_space=pl.ANY)] * (1 + n_dims),
            out_specs=[
                pl.BlockSpec((survivors // STEPS, rows, DB), lambda g, *_: (g, 0, 0)),
                pl.BlockSpec((shortlist // STEPS, rows, DB), lambda g, *_: (g, 0, 0)),
            ],
            scratch_shapes=[
                pltpu.VMEM((n_dims, n_docs, per_shard, rows, width), jnp.bfloat16),
                pltpu.VMEM((n_dims, local_blocks, DB, width), jnp.bfloat16),
                pltpu.SemaphoreType.DMA((n_dims,)),
                pltpu.SemaphoreType.DMA((n_dims,)),
            ],
        ),
        compiler_params=pltpu.CompilerParams(vmem_limit_bytes=56 * 2**20),
        cost_estimate=pl.CostEstimate(
            flops=2 * rows * DB * (shortlist * D + survivors * PREFIX),
            bytes_accessed=moved,
            transcendentals=0,
        ),
    )(surv_pairs[0], surv_count, short_pairs[0], short_count, every_query, *doc_parts)
    return (prefix_out[None], full_out[None])


def solution(mesh):
    placed = (
        P("docs", "dims"),
        P("docs", "dims"),
        P("docs", None),
        P("docs"),
        P("docs", None),
        P("docs"),
    )
    return jax.shard_map(
        functools.partial(shards, mesh.shape["dims"]),
        mesh=mesh,
        in_specs=placed,
        out_specs=(P("docs", None, "dims", None), P("docs", None, "dims", None)),
        check_vma=False,
    )
```

```python
import functools

import jax
import jax.numpy as jnp
from jax import lax
from jax.experimental import pallas as pl
from jax.experimental.pallas import tpu as pltpu
from jax.sharding import PartitionSpec as P

D = 3072
PREFIX = 768
QB = 128
DB = 128
STEPS = 6


def scores(
    n_dims, local_blocks, surv_ref, surv_n_ref, short_ref, short_n_ref, *refs
):
    query_hbm, doc_hbm = refs[0], refs[1 : 1 + n_dims]
    prefix_ref, full_ref, query_vmem, doc_vmem, query_sem, doc_sem = refs[1 + n_dims :]
    width = doc_vmem.shape[-1]
    per_shard = query_vmem.shape[2]
    step = pl.program_id(0)
    me = lax.axis_index("dims")

    early = [j for j in range(n_dims) if j * width < PREFIX]
    late = [j for j in range(n_dims) if j * width >= PREFIX]

    def query_copy(j):
        shift = lax.rem(me - j + n_dims, n_dims)
        return pltpu.make_async_copy(
            query_hbm.at[:, shift], query_vmem.at[j], query_sem.at[j]
        )

    def doc_copy(j, shift):
        return pltpu.make_async_copy(doc_hbm[shift], doc_vmem.at[j], doc_sem.at[j])

    def start(places):
        for j in places:
            query_copy(j).start()
            for shift in range(n_dims):

                @pl.when(lax.rem(me - j + n_dims, n_dims) == shift)
                def _(j=j, shift=shift):
                    doc_copy(j, shift).start()

    def wait(places):
        for j in places:
            query_copy(j).wait()
            doc_copy(j, 0).wait()

    @pl.when(step == 0)
    def _():
        start(early)
        wait(early)
        start(late)

    @pl.when(step == STEPS)
    def _():
        wait(late)

    def slots(at, pair_ref, count_ref, out_ref, columns):
        per_step = out_ref.shape[0]
        for i in range(per_step):
            slot = at * per_step + i
            pair = pair_ref[slot]
            query_block = pair // local_blocks
            doc_block = pair % local_blocks
            total = None
            for j in range(n_dims):
                used = min(max(columns - j * width, 0), width)
                if used == 0:
                    continue
                term = lax.dot_general(
                    query_vmem[j, query_block // per_shard, query_block % per_shard, :, :used],
                    doc_vmem[j, doc_block, :, :used],
                    (((1,), (1,)), ((), ())),
                    preferred_element_type=jnp.float32,
                )
                total = term if total is None else total + term
            scaled = total * (float(columns) ** -0.5)
            out_ref[i] = jnp.where(slot < count_ref[0], scaled, jnp.float32(0.0))

    @pl.when(step < STEPS)
    def _():
        slots(step, surv_ref, surv_n_ref, prefix_ref, PREFIX)

    @pl.when(step >= STEPS)
    def _():
        slots(step - STEPS, short_ref, short_n_ref, full_ref, D)


def shards(
    n_dims, queries, doc_vectors, surv_pairs, surv_count, short_pairs, short_count
):
    width = queries.shape[1]
    rows = QB // n_dims
    local_blocks = doc_vectors.shape[0] // DB
    me = lax.axis_index("dims")
    by_rows = queries.reshape(-1, n_dims, rows, width)
    docs = doc_vectors.reshape(local_blocks, DB, width)
    query_parts, doc_parts = [], []
    for shift in range(n_dims):
        target = lax.rem(me + shift, n_dims)
        part = lax.dynamic_index_in_dim(by_rows, target, 1, keepdims=False)
        doc_part = docs
        if shift:
            pairs = [(i, (i + shift) % n_dims) for i in range(n_dims)]
            part = lax.ppermute(part, "dims", pairs)
            doc_part = lax.ppermute(docs, "dims", pairs)
        query_parts.append(part)
        doc_parts.append(doc_part)
    every_query = lax.all_gather(jnp.stack(query_parts), "docs", axis=0, tiled=False)
    n_docs, _, per_shard = every_query.shape[:3]
    blocks = n_docs * per_shard
    survivors, shortlist = surv_pairs.shape[1], short_pairs.shape[1]
    outs = [
        jax.ShapeDtypeStruct((survivors, rows, DB), jnp.float32),
        jax.ShapeDtypeStruct((shortlist, rows, DB), jnp.float32),
    ]
    moved = 2 * (blocks * rows + local_blocks * DB) * D + 4 * (survivors + shortlist) * rows * DB
    prefix_out, full_out = pl.pallas_call(
        functools.partial(scores, n_dims, local_blocks),
        out_shape=outs,
        grid_spec=pltpu.PrefetchScalarGridSpec(
            num_scalar_prefetch=4,
            grid=(2 * STEPS,),
            in_specs=[pl.BlockSpec(memory_space=pl.ANY)] * (1 + n_dims),
            out_specs=[
                pl.BlockSpec((survivors // STEPS, rows, DB), lambda g, *_: (jnp.minimum(g, STEPS - 1), 0, 0)),
                pl.BlockSpec((shortlist // STEPS, rows, DB), lambda g, *_: (jnp.maximum(g - STEPS, 0), 0, 0)),
            ],
            scratch_shapes=[
                pltpu.VMEM((n_dims, n_docs, per_shard, rows, width), jnp.bfloat16),
                pltpu.VMEM((n_dims, local_blocks, DB, width), jnp.bfloat16),
                pltpu.SemaphoreType.DMA((n_dims,)),
                pltpu.SemaphoreType.DMA((n_dims,)),
            ],
        ),
        compiler_params=pltpu.CompilerParams(vmem_limit_bytes=56 * 2**20),
        cost_estimate=pl.CostEstimate(
            flops=2 * rows * DB * (shortlist * D + survivors * PREFIX),
            bytes_accessed=moved,
            transcendentals=0,
        ),
    )(surv_pairs[0], surv_count, short_pairs[0], short_count, every_query, *doc_parts)
    return (prefix_out[None], full_out[None])


def solution(mesh):
    placed = (
        P("docs", "dims"),
        P("docs", "dims"),
        P("docs", None),
        P("docs"),
        P("docs", None),
        P("docs"),
    )
    return jax.shard_map(
        functools.partial(shards, mesh.shape["dims"]),
        mesh=mesh,
        in_specs=placed,
        out_specs=(P("docs", None, "dims", None), P("docs", None, "dims", None)),
        check_vma=False,
    )
```
